32 devices in a mesh: blk: 4 (over y, x), dom: 8 (over z, core).
Axes of the slice: x: 2, y: 2, z: 4, core: 2. Of those that a mesh axis runs over, the one named last changes fastest.
Arguments:
- source_emb: bfloat16 [4096, 64], P(('blk', 'dom')), may hold values from -6 to 6
- target_emb: bfloat16 [24576, 64], P(('blk', 'dom')), may hold values from -6 to 6
- source_counts: int32 [4096, 128], P(('blk', 'dom')), may hold values from 1 to 4
- target_counts: int32 [24576, 128], P(('blk', 'dom')), may hold values from 1 to 4
- warm_start: float32 [24576, 128], P(('blk', 'dom')), may hold values from -8 to 263
Outputs:
- source_log_scaling: float32 [4096, 128], P(('blk', 'dom'))
- target_log_scaling: float32 [24576, 128], P(('blk', 'dom'))
The draws below stay inside these ranges and needn't reach their ends.
All inputs are finite; a program needn't handle non-finite values.
Results may differ from the reference program's by a relative error of at most 0.0022.
Values may be sent and summed in bfloat16 or wider, within the bound.
A program may use at most 64 MiB of HBM per device.

```python
import math
import jax
import jax.numpy as jnp
from jax import lax

D = 64
B = 128
ITERS = 2
NS = 4096
NT = 24576


def draw_warm_start(key, part):
    first_key = jax.random.fold_in(key, 0)
    return jnp.clip(2.0 * jax.random.normal(first_key, (NT, B), jnp.float32), -8.0, 8.0)


def place_ends(values, own_key, smallest, largest):
    shape = values.shape
    index_at = [jax.random.randint(jax.random.fold_in(own_key, axis), (), 0, shape[axis]) for axis in range(len(shape))]
    values = values.at[tuple(index_at)].set(smallest)
    longest = shape.index(max(shape))
    index_at[longest] = (index_at[longest] + 1) % shape[longest]
    return values.at[tuple(index_at)].set(largest)


def steps_of(stream_key, extent, cuts, least, high):
    def one(position, shards_of):
        heights = jax.random.uniform(jax.random.fold_in(jax.random.fold_in(stream_key, 6), position), (shards_of,), jnp.float32, least / len(cuts), high / len(cuts))
        return jnp.repeat(jnp.exp(heights), extent[position] // shards_of).reshape((-1,) + (1,) * (len(extent) - position - 1))

    gain = one(*cuts[0])
    for cut in cuts[1:]:
        gain = gain * one(*cut)
    return gain


def centred(rng, dims, scale, reach, pieces=(), dtype=jnp.bfloat16):
    gain = steps_of(rng, dims, pieces, -0.22, 0.18) if pieces else 1.0
    array = jax.random.normal(rng, dims, jnp.float32) * scale * gain
    return jnp.minimum(jnp.maximum(array, -reach), reach).astype(dtype)


def setup_inputs(seed: int = 0) -> dict:
    splits = jax.random.split(jax.random.key(seed), 6)
    source_emb = centred(splits[0], (NS, D), 1.0, 6.0, ((0, 32),))
    target_emb = centred(splits[1], (NT, D), 1.0, 6.0, ((0, 32),))
    source_counts = place_ends(jax.random.randint(splits[2], (NS, B), 1, 5), jax.random.fold_in(splits[2], 1), 1, 4).astype(jnp.int32)
    target_counts = place_ends(jax.random.randint(splits[3], (NT, B), 1, 5), jax.random.fold_in(splits[3], 1), 1, 4).astype(jnp.int32)
    warm_start = draw_warm_start(jax.random.fold_in(splits[5], 71), 0)
    return {"source_emb": source_emb, "target_emb": target_emb, "source_counts": source_counts, "target_counts": target_counts, "warm_start": warm_start}


entropic = 0.05

def normalized(values):
    widened = values.astype(jnp.float32)
    squared = lax.optimization_barrier(jnp.sum(widened * widened, axis=1, keepdims=True)) + 1e-06
    return (widened * lax.rsqrt(squared)).astype(jnp.bfloat16)

def kernel_sums(row_emb, col_emb, col_weights):
    row_count = row_emb.shape[0]
    col_count = col_emb.shape[0]
    row_block = math.gcd(row_count, 512)
    col_block = math.gcd(col_count, 2048)
    row_parts = row_emb.reshape(row_count // row_block, row_block, row_emb.shape[1])
    col_parts = col_emb.reshape(col_count // col_block, col_block, col_emb.shape[1])
    weight_parts = col_weights.reshape(col_count // col_block, col_block, col_weights.shape[1])

    def one_block(row_piece):

        def add_block(running, paired):
            col_piece, weight_piece = paired
            products = jnp.dot(row_piece, col_piece.T, preferred_element_type=jnp.float32)
            kernel = jnp.exp((products - 1.0) / entropic).astype(jnp.bfloat16)
            return (running + jnp.dot(kernel, weight_piece, preferred_element_type=jnp.float32), None)
        initial = jnp.zeros((row_piece.shape[0], col_weights.shape[1]), jnp.float32)
        result, unused = lax.scan(add_block, initial, (col_parts, weight_parts))
        return result
    return lax.map(one_block, row_parts).reshape(row_count, col_weights.shape[1])

def reference(source_emb, target_emb, source_counts, target_counts, warm_start):
    source_unit = normalized(source_emb)
    target_unit = normalized(target_emb)
    log_source = jnp.log(source_counts.astype(jnp.float32)) - math.log(NS)
    log_target = jnp.log(target_counts.astype(jnp.float32)) - math.log(NT)
    target_logs = warm_start
    source_logs = jnp.zeros((NS, B), jnp.float32)
    for iteration in range(ITERS):
        target_peak = lax.optimization_barrier(jnp.max(target_logs, axis=0))
        target_weights = jnp.exp(target_logs - target_peak).astype(jnp.bfloat16)
        source_sums = kernel_sums(source_unit, target_unit, target_weights)
        source_logs = log_source - target_peak - jnp.log(source_sums)
        source_peak = lax.optimization_barrier(jnp.max(source_logs, axis=0))
        source_weights = jnp.exp(source_logs - source_peak).astype(jnp.bfloat16)
        target_sums = kernel_sums(target_unit, source_unit, source_weights)
        target_logs = log_target - source_peak - jnp.log(target_sums)
    return (source_logs, target_logs)
```

```python
import functools
import math

import jax
import jax.numpy as jnp
from jax import lax
from jax.experimental import pallas as pl
from jax.experimental.pallas import tpu as pltpu
from jax.sharding import PartitionSpec as P

ITERS = 2
INV_EPS = 20.0
LOG2E = math.log2(math.e)
CHUNK = 128


def normalized(values):
    widened = values.astype(jnp.float32)
    squared = jnp.sum(widened * widened, axis=1, keepdims=True) + 1e-06
    return widened * lax.rsqrt(squared)


def kernel(nb, nz, *refs):
    (semb, temb, scnt, tcnt, warm, sout, tout,
     S, tt, tt2, warm2, peak, K, W, VT, tsT, part_out, part_in, z_out, z_in,
     ts_out, ts_in, ssem, rsem) = refs
    src = semb.shape[0]
    tgt = temb.shape[0]
    cols = warm.shape[1]
    slab = src * nz
    b = lax.axis_index("blk")
    d = lax.axis_index("dom")
    z = d // 2
    c = d % 2
    count = [0]

    core_peer = (b, 2 * z + 1 - c)

    def z_peer(k):
        return (b, 2 * lax.rem(z + k, nz) + c)

    def b_peer(k):
        return (lax.rem(b + k, nb), d)

    started = []

    def send(source, target, device):
        i = count[0]
        count[0] += 1
        copy = pltpu.make_async_remote_copy(
            src_ref=source, dst_ref=target, send_sem=ssem.at[i], recv_sem=rsem.at[i],
            device_id=device, device_id_type=pl.DeviceIdType.MESH)
        copy.start()
        started.append(copy)
        return copy

    barrier = pltpu.get_barrier_semaphore()
    peers = [core_peer] + [z_peer(k) for k in range(1, nz)] + [b_peer(k) for k in range(1, nb)]
    for device in peers:
        pl.semaphore_signal(barrier, inc=1, device_id=device, device_id_type=pl.DeviceIdType.MESH)

    own_block = b * nz + z
    my_rows = pl.ds(pl.multiple_of(own_block * src, src), src)
    S[my_rows, :] = normalized(semb[...]).astype(jnp.bfloat16)
    peak[0] = jnp.broadcast_to(jnp.max(warm[...], axis=0, keepdims=True), (8, cols))
    tt[...] = normalized(temb[...]).T.astype(jnp.bfloat16)
    pl.semaphore_wait(barrier, len(peers))

    emb_z, peak_z = [], []
    for k in range(1, nz):
        emb_z.append(send(S.at[my_rows], S.at[my_rows], z_peer(k)))
        peak_z.append(send(peak.at[0], peak.at[k], z_peer(k)))
    emb_core = send(tt, tt2, core_peer)
    warm_core = send(warm, warm2, core_peer)

    def slab_rows(block):
        return pl.ds(pl.multiple_of(block * slab, slab), slab)

    for copy in peak_z:
        copy.wait_recv()
    top = peak[0]
    for k in range(1, nz):
        top = jnp.maximum(top, peak[k])
    peak[nz] = top
    peak_b = [send(peak.at[nz], peak.at[nz + k], b_peer(k)) for k in range(1, nb)]
    for copy in emb_z:
        copy.wait_recv()
    own_rows = slab_rows(b)
    emb_b = [send(S.at[own_rows], S.at[own_rows], b_peer(k)) for k in range(1, nb)]
    emb_core.wait_recv()

    width = next(w for w in (384, 256, 128) if tgt % w == 0)
    steps = slab // CHUNK
    scale = INV_EPS * LOG2E

    def make_kernel(block, out_slot):
        base = block * slab

        def one(step, carry):
            rows = pl.ds(pl.multiple_of(base + step * CHUNK, CHUNK), CHUNK)
            piece = S[rows, :]
            total = None
            for half, emb in enumerate((tt, tt2)):
                for start in range(0, tgt, width):
                    prod = jnp.dot(piece, emb[:, start:start + width], preferred_element_type=jnp.float32)
                    kern = jnp.exp2((prod - 1.0) * scale).astype(jnp.bfloat16)
                    at = half * tgt + start
                    K[rows, at:at + width] = kern
                    if out_slot is not None:
                        term = jnp.dot(kern, W[at:at + width, :], preferred_element_type=jnp.float32)
                        total = term if total is None else total + term
            if out_slot is not None:
                part_out[out_slot, pl.ds(pl.multiple_of(step * CHUNK, CHUNK), CHUNK), :] = total.astype(jnp.bfloat16)
            return carry

        lax.fori_loop(0, steps, one, 0)

    def source_part(block, out_slot):
        base = block * slab

        def one(step, carry):
            rows = pl.ds(pl.multiple_of(base + step * CHUNK, CHUNK), CHUNK)
            total = jnp.dot(K[rows, :], W[...], preferred_element_type=jnp.float32)
            part_out[out_slot, pl.ds(pl.multiple_of(step * CHUNK, CHUNK), CHUNK), :] = total.astype(jnp.bfloat16)
            return carry

        lax.fori_loop(0, steps, one, 0)

    make_kernel(b, None)

    for copy in peak_b:
        copy.wait_recv()
    top = peak[nz]
    for k in range(1, nb):
        top = jnp.maximum(top, peak[nz + k])
    peak[nz + nb] = top
    peak_core = send(peak.at[nz + nb], peak.at[nz + nb + 1], core_peer)
    warm_core.wait_recv()
    peak_core.wait_recv()
    shift = jnp.maximum(peak[nz + nb], peak[nz + nb + 1])[0:1, :]
    W[0:tgt, :] = jnp.exp(warm[...] - shift).astype(jnp.bfloat16)
    W[tgt:2 * tgt, :] = jnp.exp(warm2[...] - shift).astype(jnp.bfloat16)

    log_ns = math.log(src * nb * nz * 2)
    log_nt = math.log(tgt * nb * nz * 2)
    inv_ns = 1.0 / (src * nb * nz * 2)
    inv_nt = 1.0 / (tgt * nb * nz * 2)

    for it in range(ITERS):
        last = it == ITERS - 1
        slot0 = it * (nb - 1)
        sent = []
        for k in range(1, nb):
            block = lax.rem(b + k, nb)
            slot = slot0 + k - 1
            if it == 0:
                emb_b[nb - k - 1].wait_recv()
                make_kernel(block, it * nb + k)
            else:
                source_part(block, it * nb + k)
            sent.append(send(part_out.at[it * nb + k], part_in.at[slot], b_peer(k)))
        source_part(b, it * nb)
        for copy in sent:
            copy.wait_recv()
        zslot = it * nz

        def summed(block):
            rows = pl.ds(pl.multiple_of(block * src, src), src)
            total = part_out[it * nb, rows, :].astype(jnp.float32)
            for k in range(nb - 1):
                total = total + part_in[slot0 + k, rows, :].astype(jnp.float32)
            return total

        sent = []
        for k in range(1, nz):
            z_out[zslot + k] = summed(lax.rem(z + k, nz)).astype(jnp.bfloat16)
            sent.append(send(z_out.at[zslot + k], z_in.at[zslot + k], z_peer(k)))
        sums = summed(z)
        for copy in sent:
            copy.wait_recv()
        for k in range(1, nz):
            sums = sums + z_in[zslot + k].astype(jnp.float32)
        counts = scnt[...].astype(jnp.float32)
        vt = VT.at[it]
        vt[own_block] = (counts * inv_ns / sums).T.astype(jnp.bfloat16)
        sent = [send(vt.at[own_block], vt.at[own_block], z_peer(k)) for k in range(1, nz)]
        if last:
            sout[...] = jnp.log(counts) - log_ns - shift - jnp.log(sums)
        for copy in sent:
            copy.wait_recv()
        mine = pl.ds(b * nz, nz)
        sent = [send(vt.at[mine], vt.at[mine], b_peer(k)) for k in range(1, nb)]

        def weights(block):
            return jnp.concatenate([vt[block * nz + i] for i in range(nz)], axis=1)

        tsT[...] = jnp.dot(weights(b), K[slab_rows(b), :], preferred_element_type=jnp.float32)
        for k in range(1, nb):
            sent[k - 1].wait_recv()
            block = lax.rem(b - k + nb, nb)
            lhs = weights(block)
            if k < nb - 1:
                tsT[...] += jnp.dot(lhs, K[slab_rows(block), :], preferred_element_type=jnp.float32)
            else:
                ts_out[it] = (tsT[:, tgt:] + jnp.dot(
                    lhs, K[slab_rows(block), tgt:], preferred_element_type=jnp.float32)).astype(jnp.bfloat16)
                across = send(ts_out.at[it], ts_in.at[it], core_peer)
                tsT[:, :tgt] += jnp.dot(lhs, K[slab_rows(block), :tgt], preferred_element_type=jnp.float32)
        across.wait_recv()
        tsums = (tsT[:, :tgt] + ts_in[it].astype(jnp.float32)).T
        tcounts = tcnt[...].astype(jnp.float32)
        if last:
            tout[...] = jnp.log(tcounts) - log_nt + shift - jnp.log(tsums)
        else:
            W2 = W
            W2[0:tgt, :] = (tcounts * inv_nt / tsums).astype(jnp.bfloat16)
            across = send(W2.at[0:tgt], W2.at[tgt:2 * tgt], core_peer)
            across.wait_recv()
    for copy in started:
        copy.wait_send()


def n_copies(nb, nz):
    return 2 * (nz - 1) + 2 + 2 * (nb - 1) + 1 + ITERS * (2 * (nb - 1) + 2 * (nz - 1) + 1) + ITERS - 1


def body(source_emb, target_emb, source_counts, target_counts, warm_start):
    nb = lax.axis_size("blk")
    nz = lax.axis_size("dom") // 2
    src, dim = source_emb.shape
    tgt = target_emb.shape[0]
    cols = warm_start.shape[1]
    slab = src * nz
    copies = n_copies(nb, nz)
    bf = jnp.bfloat16
    f32 = jnp.float32
    vmem = pltpu.VMEM
    pairs = slab * nb * 2 * tgt
    return pl.pallas_call(
        functools.partial(kernel, nb, nz),
        out_shape=(jax.ShapeDtypeStruct((src, cols), f32), jax.ShapeDtypeStruct((tgt, cols), f32)),
        in_specs=[pl.BlockSpec(memory_space=pltpu.VMEM)] * 5,
        out_specs=(pl.BlockSpec(memory_space=pltpu.VMEM),) * 2,
        scratch_shapes=[
            vmem((slab * nb, dim), bf),
            vmem((dim, tgt), bf),
            vmem((dim, tgt), bf),
            vmem((tgt, cols), f32),
            vmem((nz + nb + 2, 8, cols), f32),
            vmem((slab * nb, 2 * tgt), bf),
            vmem((2 * tgt, cols), bf),
            vmem((ITERS, nb * nz, cols, src), bf),
            vmem((cols, 2 * tgt), f32),
            vmem((ITERS * nb, slab, cols), bf),
            vmem((ITERS * (nb - 1), slab, cols), bf),
            vmem((ITERS * nz, src, cols), bf),
            vmem((ITERS * nz, src, cols), bf),
            vmem((ITERS, cols, tgt), bf),
            vmem((ITERS, cols, tgt), bf),
            pltpu.SemaphoreType.DMA((copies,)),
            pltpu.SemaphoreType.DMA((copies,)),
        ],
        cost_estimate=pl.CostEstimate(
            flops=2 * pairs * (dim + 4 * cols), bytes_accessed=2 * 10**6, transcendentals=pairs),
        compiler_params=pltpu.CompilerParams(
            collective_id=0, has_side_effects=True, vmem_limit_bytes=56 * 2**20),
    )(source_emb, target_emb, source_counts, target_counts, warm_start)


def solution(mesh):
    spec = P(("blk", "dom"), None)
    return jax.shard_map(
        body, mesh=mesh, in_specs=(spec,) * 5, out_specs=(spec,) * 2, check_vma=False)
```

```python
import functools
import math

import jax
import jax.numpy as jnp
from jax import lax
from jax.experimental import pallas as pl
from jax.experimental.pallas import tpu as pltpu
from jax.sharding import PartitionSpec as P

ITERS = 2
INV_EPS = 20.0
LOG2E = math.log2(math.e)


def normalized(values):
    widened = values.astype(jnp.float32)
    squared = jnp.sum(widened * widened, axis=0, keepdims=True) + 1e-06
    return widened * lax.rsqrt(squared)


def kernel(nb, nz, *refs):
    (semb, temb, scnt, tcnt, warm, sout, tout,
     S, tt, tt2, warm2, peak, K, W, VT, tsT, part_out, part_in, z_out, z_in,
     ts_out, ts_in, ssem, rsem) = refs
    src = semb.shape[1]
    tgt = temb.shape[1]
    cols = warm.shape[1]
    group = src * nb
    b = lax.axis_index("blk")
    d = lax.axis_index("dom")
    z = d // 2
    c = d % 2
    count = [0]
    f32, bf = jnp.float32, jnp.bfloat16

    core_peer = (b, 2 * z + 1 - c)

    def z_peer(k):
        return (b, 2 * lax.rem(z + k, nz) + c)

    def b_peer(k):
        return (lax.rem(b + k, nb), d)

    started = []

    def send(source, target, device):
        i = count[0]
        count[0] += 1
        copy = pltpu.make_async_remote_copy(
            src_ref=source, dst_ref=target, send_sem=ssem.at[i], recv_sem=rsem.at[i],
            device_id=device, device_id_type=pl.DeviceIdType.MESH)
        copy.start()
        started.append(copy)
        return copy

    def arrived(copies):
        for copy in copies:
            copy.wait_recv()

    barrier = pltpu.get_barrier_semaphore()
    peers = [core_peer] + [z_peer(k) for k in range(1, nz)] + [b_peer(k) for k in range(1, nb)]
    for device in peers:
        pl.semaphore_signal(barrier, inc=1, device_id=device, device_id_type=pl.DeviceIdType.MESH)

    def group_of(i):
        return lax.rem(z - i + nz, nz)

    def block_rows(i):
        return pl.ds(pl.multiple_of((group_of(i) * nb + b) * src, src), src)

    def group_rows(i):
        return pl.ds(pl.multiple_of(group_of(i) * group, group), group)

    S[block_rows(0), :] = normalized(semb[...]).T.astype(bf)
    peak[0] = jnp.broadcast_to(jnp.max(warm[...], axis=0, keepdims=True), (8, cols))
    tt[...] = normalized(temb[...]).astype(bf)
    pl.semaphore_wait(barrier, len(peers))

    mine = S.at[block_rows(0)]
    emb_z = [send(mine, mine, z_peer(k)) for k in range(1, nz)]
    peak_z = [send(peak.at[0], peak.at[k], z_peer(k)) for k in range(1, nz)]
    emb_core = send(tt, tt2, core_peer)
    emb_b = [[send(mine, mine, b_peer(j)) for j in range(1, nb)]]
    warm_core = send(warm, warm2, core_peer)

    arrived(peak_z)
    top = peak[0]
    for k in range(1, nz):
        top = jnp.maximum(top, peak[k])
    peak[nz] = top
    peak_b = [send(peak.at[nz], peak.at[nz + k], b_peer(k)) for k in range(1, nb)]
    for k in range(1, nz):
        emb_z[k - 1].wait_recv()
        piece = S.at[block_rows(k)]
        emb_b.append([send(piece, piece, b_peer(j)) for j in range(1, nb)])
    emb_core.wait_recv()

    width = 256 if tgt % 256 == 0 else 128
    tall = 256 if group % 256 == 0 else 128
    scale = INV_EPS * LOG2E

    def make_kernel(i):
        base = group_of(i) * group

        def one(step, carry):
            rows = pl.ds(pl.multiple_of(base + step * tall, tall), tall)
            piece = S[rows, :]
            for half, emb in enumerate((tt, tt2)):
                for start in range(0, tgt, width):
                    prod = jnp.dot(piece, emb[:, start:start + width], preferred_element_type=f32)
                    at = half * tgt + start
                    K[rows, at:at + width] = jnp.exp2((prod - 1.0) * scale).astype(bf)
            return carry

        lax.fori_loop(0, group // tall, one, 0)

    arrived(emb_b[0])
    make_kernel(0)
    arrived(peak_b)
    top = peak[nz]
    for k in range(1, nb):
        top = jnp.maximum(top, peak[nz + k])
    peak[nz + nb] = top
    peak_core = send(peak.at[nz + nb], peak.at[nz + nb + 1], core_peer)
    if nz > 1:
        arrived(emb_b[1])
        make_kernel(1)
    warm_core.wait_recv()
    peak_core.wait_recv()
    shift = jnp.maximum(peak[nz + nb], peak[nz + nb + 1])[0:1, :]
    W[0:tgt, :] = jnp.exp(warm[...] - shift).astype(bf)
    W[tgt:2 * tgt, :] = jnp.exp(warm2[...] - shift).astype(bf)

    all_src = src * nb * nz * 2
    all_tgt = tgt * nb * nz * 2

    for it in range(ITERS):
        last = it == ITERS - 1
        to_b = [None] * (nz + 1)

        def scatter(i):
            part = part_out.at[it * nz + i % nz]
            part[...] = jnp.dot(K[group_rows(i), :], W[...], preferred_element_type=f32).astype(bf)
            to_b[i] = []
            for j in range(1, nb):
                rows = pl.ds(pl.multiple_of(lax.rem(b + j, nb) * src, src), src)
                to_b[i].append(send(part.at[rows], part_in.at[(it * nz + i % nz) * (nb - 1) + j - 1], b_peer(j)))

        def summed(i):
            arrived(to_b[i])
            slot = it * nz + i % nz
            total = part_out[slot, pl.ds(pl.multiple_of(b * src, src), src), :].astype(f32)
            for j in range(nb - 1):
                total = total + part_in[slot * (nb - 1) + j].astype(f32)
            return total

        to_z = []

        def pass_on(i):
            slot = it * nz + i
            z_out[slot] = summed(i).astype(bf)
            to_z.append(send(z_out.at[slot], z_in.at[slot], z_peer(nz - i)))

        for i in range(1, nz + 1):
            if it == 0 and 1 < i < nz:
                arrived(emb_b[i])
                make_kernel(i)
            scatter(i)
            if it == 0 and i > 1:
                pass_on(i - 1)
        if it > 0:
            for i in range(1, nz):
                pass_on(i)
        sums = summed(nz)
        arrived(to_z)
        for i in range(1, nz):
            sums = sums + z_in[it * nz + i].astype(f32)
        counts = scnt[...].astype(f32)
        vt = VT.at[it]

        def block(i):
            return vt.at[group_of(i) * nb + b]

        vt[group_of(0) * nb + b] = (counts * (1.0 / all_src) / sums).T.astype(bf)
        from_z = [send(block(0), block(0), z_peer(k)) for k in range(1, nz)]
        from_b = [[send(block(0), block(0), b_peer(j)) for j in range(1, nb)]]
        if last:
            sout[...] = jnp.log(counts) - math.log(all_src) - shift - jnp.log(sums)
        for k in range(1, nz):
            from_z[k - 1].wait_recv()
            from_b.append([send(block(k), block(k), b_peer(j)) for j in range(1, nb)])
        for i in range(nz):
            arrived(from_b[i])
            first = group_of(i) * nb
            lhs = jnp.concatenate([vt[first + j] for j in range(nb)], axis=1)
            for half in (1, 0):
                at = half * tgt
                term = jnp.dot(lhs, K[group_rows(i), at:at + tgt], preferred_element_type=f32)
                if i > 0:
                    term = term + tsT[:, at:at + tgt]
                if i == nz - 1 and half == 1:
                    ts_out[it] = term.astype(bf)
                    across = send(ts_out.at[it], ts_in.at[it], core_peer)
                else:
                    tsT[:, at:at + tgt] = term
        tcounts = tcnt[...].astype(f32)
        across.wait_recv()
        tsums = (tsT[:, :tgt] + ts_in[it].astype(f32)).T
        if last:
            tout[...] = jnp.log(tcounts) - math.log(all_tgt) + shift - jnp.log(tsums)
        else:
            W[0:tgt, :] = (tcounts * (1.0 / all_tgt) / tsums).astype(bf)
            send(W.at[0:tgt], W.at[tgt:2 * tgt], core_peer).wait_recv()
    for copy in started:
        copy.wait_send()


def n_copies(nb, nz):
    gather = (nz - 1) + (nb - 1) * nz
    return gather + (nz - 1) + (nb - 1) + 3 + ITERS * (gather + nz * (nb - 1) + nz - 1 + 1) + ITERS - 1


def place(s_in, t_in, s_out, t_out, sem):
    copies = [pltpu.make_async_copy(s_in, s_out, sem.at[0]), pltpu.make_async_copy(t_in, t_out, sem.at[1])]
    for copy in copies:
        copy.start()
    for copy in copies:
        copy.wait()


def body(source_emb, target_emb, source_counts, target_counts, warm_start):
    nb = lax.axis_size("blk")
    nz = lax.axis_size("dom") // 2
    src, dim = source_emb.shape
    tgt = target_emb.shape[0]
    cols = warm_start.shape[1]
    group = src * nb
    copies = n_copies(nb, nz)
    bf = jnp.bfloat16
    f32 = jnp.float32
    vmem = pltpu.VMEM
    pairs = group * nz * 2 * tgt
    shapes = (jax.ShapeDtypeStruct((src, cols), f32), jax.ShapeDtypeStruct((tgt, cols), f32))
    results = pl.pallas_call(
        functools.partial(kernel, nb, nz),
        out_shape=shapes,
        in_specs=[pl.BlockSpec(memory_space=pltpu.VMEM)] * 5,
        out_specs=(pl.BlockSpec(memory_space=pltpu.VMEM),) * 2,
        scratch_shapes=[
            vmem((group * nz, dim), bf),
            vmem((dim, tgt), bf),
            vmem((dim, tgt), bf),
            vmem((tgt, cols), f32),
            vmem((nz + nb + 2, 8, cols), f32),
            vmem((group * nz, 2 * tgt), bf),
            vmem((2 * tgt, cols), bf),
            vmem((ITERS, nb * nz, cols, src), bf),
            vmem((cols, 2 * tgt), f32),
            vmem((ITERS * nz, group, cols), bf),
            vmem((ITERS * nz * (nb - 1), src, cols), bf),
            vmem((ITERS * nz, src, cols), bf),
            vmem((ITERS * nz, src, cols), bf),
            vmem((ITERS, cols, tgt), bf),
            vmem((ITERS, cols, tgt), bf),
            pltpu.SemaphoreType.DMA((copies,)),
            pltpu.SemaphoreType.DMA((copies,)),
        ],
        cost_estimate=pl.CostEstimate(
            flops=2 * pairs * (dim + 4 * cols), bytes_accessed=2 * 10**6, transcendentals=pairs),
        compiler_params=pltpu.CompilerParams(
            collective_id=0, has_side_effects=True, vmem_limit_bytes=56 * 2**20),
    )(source_emb.T, target_emb.T, source_counts, target_counts, warm_start)
    return pl.pallas_call(
        place,
        out_shape=shapes,
        in_specs=[pl.BlockSpec(memory_space=pltpu.HBM)] * 2,
        out_specs=(pl.BlockSpec(memory_space=pl.ANY),) * 2,
        scratch_shapes=[pltpu.SemaphoreType.DMA((2,))],
    )(*results)


def solution(mesh):
    spec = P(("blk", "dom"), None)
    return jax.shard_map(
        body, mesh=mesh, in_specs=(spec,) * 5, out_specs=(spec,) * 2, check_vma=False)
```

```python
import functools
import math

import jax
import jax.numpy as jnp
from jax import lax
from jax.experimental import pallas as pl
from jax.experimental.pallas import tpu as pltpu
from jax.sharding import PartitionSpec as P

ITERS = 2
INV_EPS = 20.0
LOG2E = math.log2(math.e)


def normalized(values):
    widened = values.astype(jnp.float32)
    squared = jnp.sum(widened * widened, axis=0, keepdims=True) + 1e-06
    return widened * lax.rsqrt(squared)


def kernel(nb, nz, *refs):
    (semb, temb, scnt, tcnt, warm, sout, tout,
     S, tt, tt2, warm2, tcnt2, peak, K, W, VT, tsT, part_out, part_in, z_out, z_in,
     ts_out, ts_in, ssem, rsem) = refs
    src = semb.shape[1]
    tgt = temb.shape[1]
    cols = warm.shape[1]
    group = src * nb
    b = lax.axis_index("blk")
    d = lax.axis_index("dom")
    z = d // 2
    c = d % 2
    count = [0]
    f32, bf = jnp.float32, jnp.bfloat16

    core_peer = (b, 2 * z + 1 - c)

    def z_peer(k):
        return (b, 2 * lax.rem(z + k, nz) + c)

    def b_peer(k):
        return (lax.rem(b + k, nb), d)

    started = []

    def send(source, target, device):
        i = count[0]
        count[0] += 1
        copy = pltpu.make_async_remote_copy(
            src_ref=source, dst_ref=target, send_sem=ssem.at[i], recv_sem=rsem.at[i],
            device_id=device, device_id_type=pl.DeviceIdType.MESH)
        copy.start()
        started.append(copy)
        return copy

    def arrived(copies):
        for copy in copies:
            copy.wait_recv()

    barrier = pltpu.get_barrier_semaphore()
    peers = [core_peer] + [z_peer(k) for k in range(1, nz)] + [b_peer(k) for k in range(1, nb)]
    for device in peers:
        pl.semaphore_signal(barrier, inc=1, device_id=device, device_id_type=pl.DeviceIdType.MESH)

    def group_of(i):
        return lax.rem(z - i + nz, nz)

    def block_rows(i):
        return pl.ds(pl.multiple_of((group_of(i) * nb + b) * src, src), src)

    def group_rows(i):
        return pl.ds(pl.multiple_of(group_of(i) * group, group), group)

    scaled = normalized(semb[...]).astype(bf).astype(f32).T * (INV_EPS * LOG2E)
    high = scaled.astype(bf)
    low = (scaled - high.astype(f32)).astype(bf)
    S[block_rows(0), :] = jnp.concatenate([high, low], axis=1)
    peak[0] = jnp.broadcast_to(jnp.max(warm[...], axis=0, keepdims=True), (8, cols))
    unit = normalized(temb[...]).astype(bf)
    tt[...] = jnp.concatenate([unit, unit], axis=0)
    pl.semaphore_wait(barrier, len(peers))

    mine = S.at[block_rows(0)]
    emb_z = [send(mine, mine, z_peer(k)) for k in range(1, nz)]
    peak_z = [send(peak.at[0], peak.at[k], z_peer(k)) for k in range(1, nz)]
    emb_core = send(tt, tt2, core_peer)
    emb_b = [[send(mine, mine, b_peer(j)) for j in range(1, nb)]]
    warm_core = send(warm, warm2, core_peer)
    tcnt_core = send(tcnt, tcnt2, core_peer)

    arrived(peak_z)
    top = peak[0]
    for k in range(1, nz):
        top = jnp.maximum(top, peak[k])
    peak[nz] = top
    peak_b = [send(peak.at[nz], peak.at[nz + k], b_peer(k)) for k in range(1, nb)]
    for k in range(1, nz):
        emb_z[k - 1].wait_recv()
        piece = S.at[block_rows(k)]
        emb_b.append([send(piece, piece, b_peer(j)) for j in range(1, nb)])
    emb_core.wait_recv()

    width = 256 if tgt % 256 == 0 else 128
    tall = 256 if group % 256 == 0 else 128

    def make_kernel(i):
        base = group_of(i) * group

        def one(step, carry):
            rows = pl.ds(pl.multiple_of(base + step * tall, tall), tall)
            piece = S[rows, :]
            for half, emb in enumerate((tt, tt2)):
                for start in range(0, tgt, width):
                    prod = jnp.dot(piece, emb[:, start:start + width], preferred_element_type=f32)
                    at = half * tgt + start
                    K[rows, at:at + width] = jnp.exp2(prod).astype(bf)
            return carry

        lax.fori_loop(0, group // tall, one, 0)

    arrived(emb_b[0])
    make_kernel(0)
    arrived(peak_b)
    top = peak[nz]
    for k in range(1, nb):
        top = jnp.maximum(top, peak[nz + k])
    peak[nz + nb] = top
    peak_core = send(peak.at[nz + nb], peak.at[nz + nb + 1], core_peer)
    if nz > 1:
        arrived(emb_b[1])
        make_kernel(1)
    warm_core.wait_recv()
    peak_core.wait_recv()
    shift = jnp.maximum(peak[nz + nb], peak[nz + nb + 1])[0:1, :]
    W[0:tgt, :] = jnp.exp(warm[...] - shift).astype(bf)
    W[tgt:2 * tgt, :] = jnp.exp(warm2[...] - shift).astype(bf)

    all_src = src * nb * nz * 2
    all_tgt = tgt * nb * nz * 2

    for it in range(ITERS):
        last = it == ITERS - 1
        to_b = [None] * (nz + 1)

        def scatter(i):
            part = part_out.at[it * nz + i % nz]
            part[...] = jnp.dot(K[group_rows(i), :], W[...], preferred_element_type=f32).astype(bf)
            to_b[i] = []
            for j in range(1, nb):
                rows = pl.ds(pl.multiple_of(lax.rem(b + j, nb) * src, src), src)
                to_b[i].append(send(part.at[rows], part_in.at[(it * nz + i % nz) * (nb - 1) + j - 1], b_peer(j)))

        def summed(i):
            arrived(to_b[i])
            slot = it * nz + i % nz
            total = part_out[slot, pl.ds(pl.multiple_of(b * src, src), src), :].astype(f32)
            for j in range(nb - 1):
                total = total + part_in[slot * (nb - 1) + j].astype(f32)
            return total

        to_z = []

        def pass_on(i):
            slot = it * nz + i
            z_out[slot] = summed(i).astype(bf)
            to_z.append(send(z_out.at[slot], z_in.at[slot], z_peer(nz - i)))

        for i in range(1, nz + 1):
            if it == 0 and 1 < i < nz:
                arrived(emb_b[i])
                make_kernel(i)
            scatter(i)
            if it == 0 and i > 1:
                pass_on(i - 1)
        if it > 0:
            for i in range(1, nz):
                pass_on(i)
        sums = summed(nz)
        arrived(to_z)
        for i in range(1, nz):
            sums = sums + z_in[it * nz + i].astype(f32)
        counts = scnt[...].astype(f32)
        vt = VT.at[it]

        def block(i):
            return vt.at[group_of(i) * nb + b]

        vt[group_of(0) * nb + b] = (counts * (1.0 / all_src) / sums).T.astype(bf)
        from_z = [send(block(0), block(0), z_peer(k)) for k in range(1, nz)]
        from_b = [[send(block(0), block(0), b_peer(j)) for j in range(1, nb)]]
        if last:
            sout[...] = jnp.log(counts) - math.log(all_src) - shift - (jnp.log(sums) - INV_EPS)
        for k in range(1, nz):
            from_z[k - 1].wait_recv()
            from_b.append([send(block(k), block(k), b_peer(j)) for j in range(1, nb)])
        across = []
        for i in range(nz):
            arrived(from_b[i])
            first = group_of(i) * nb
            lhs = jnp.concatenate([vt[first + j] for j in range(nb)], axis=1)
            for half in (1, 0):
                at = half * tgt
                term = jnp.dot(lhs, K[group_rows(i), at:at + tgt], preferred_element_type=f32)
                if i > 0:
                    term = term + tsT[:, at:at + tgt]
                if i == nz - 1 and (half == 1 or not last):
                    ts_out[it, half] = term.astype(bf)
                    across.append(send(ts_out.at[it, half], ts_in.at[it, 1 - half], core_peer))
                if half == 0 or i < nz - 1 or not last:
                    tsT[:, at:at + tgt] = term
        if last:
            log_counts = jnp.log(tcnt[...].astype(f32))
            arrived(across)
            tsums = (tsT[:, :tgt] + ts_in[it, 0].astype(f32)).T
            tout[...] = log_counts - math.log(all_tgt) + shift - jnp.log(tsums)
        else:
            if it == 0:
                tcnt_core.wait_recv()
            arrived(across)
            for half, held in enumerate((tcnt, tcnt2)):
                at = half * tgt
                tsums = (tsT[:, at:at + tgt] + ts_in[it, half].astype(f32)).T
                W[at:at + tgt, :] = (held[...].astype(f32) * (1.0 / all_tgt) / tsums).astype(bf)
    for copy in started:
        copy.wait_send()


def n_copies(nb, nz):
    gather = (nz - 1) + (nb - 1) * nz
    return gather + (nz - 1) + (nb - 1) + 4 + ITERS * (gather + nz * (nb - 1) + nz - 1 + 1) + ITERS - 1


def place(s_in, t_in, s_out, t_out):
    s_out[...] = s_in[...]
    t_out[...] = t_in[...]


def body(source_emb, target_emb, source_counts, target_counts, warm_start):
    nb = lax.axis_size("blk")
    nz = lax.axis_size("dom") // 2
    src, dim = source_emb.shape
    tgt = target_emb.shape[0]
    cols = warm_start.shape[1]
    group = src * nb
    copies = n_copies(nb, nz)
    bf = jnp.bfloat16
    f32 = jnp.float32
    vmem = pltpu.VMEM
    pairs = group * nz * 2 * tgt
    shapes = (jax.ShapeDtypeStruct((src, cols), f32), jax.ShapeDtypeStruct((tgt, cols), f32))
    results = pl.pallas_call(
        functools.partial(kernel, nb, nz),
        out_shape=shapes,
        in_specs=[pl.BlockSpec(memory_space=pltpu.VMEM)] * 5,
        out_specs=(pl.BlockSpec(memory_space=pltpu.VMEM),) * 2,
        scratch_shapes=[
            vmem((group * nz, 2 * dim), bf),
            vmem((2 * dim, tgt), bf),
            vmem((2 * dim, tgt), bf),
            vmem((tgt, cols), f32),
            vmem((tgt, cols), target_counts.dtype),
            vmem((nz + nb + 2, 8, cols), f32),
            vmem((group * nz, 2 * tgt), bf),
            vmem((2 * tgt, cols), bf),
            vmem((ITERS, nb * nz, cols, src), bf),
            vmem((cols, 2 * tgt), f32),
            vmem((ITERS * nz, group, cols), bf),
            vmem((ITERS * nz * (nb - 1), src, cols), bf),
            vmem((ITERS * nz, src, cols), bf),
            vmem((ITERS * nz, src, cols), bf),
            vmem((ITERS, 2, cols, tgt), bf),
            vmem((ITERS, 2, cols, tgt), bf),
            pltpu.SemaphoreType.DMA((copies,)),
            pltpu.SemaphoreType.DMA((copies,)),
        ],
        cost_estimate=pl.CostEstimate(
            flops=2 * pairs * (dim + 4 * cols), bytes_accessed=2 * 10**6, transcendentals=pairs),
        compiler_params=pltpu.CompilerParams(
            collective_id=0, has_side_effects=True, vmem_limit_bytes=56 * 2**20),
    )(source_emb.T, target_emb.T, source_counts, target_counts, warm_start)
    return pl.pallas_call(
        place,
        out_shape=shapes,
        in_specs=[pl.BlockSpec(memory_space=pltpu.VMEM)] * 2,
        out_specs=(pl.BlockSpec(memory_space=pltpu.VMEM),) * 2,
    )(*results)


def solution(mesh):
    spec = P(("blk", "dom"), None)
    return jax.shard_map(
        body, mesh=mesh, in_specs=(spec,) * 5, out_specs=(spec,) * 2, check_vma=False)
```

```python
import functools
import math

import jax
import jax.numpy as jnp
from jax import lax
from jax.experimental import pallas as pl
from jax.experimental.pallas import tpu as pltpu
from jax.sharding import PartitionSpec as P

ITERS = 2
INV_EPS = 20.0
LOG2E = math.log2(math.e)


def normalized(values):
    widened = values.astype(jnp.float32)
    squared = jnp.sum(widened * widened, axis=0, keepdims=True) + 1e-06
    return widened * lax.rsqrt(squared)


def kernel(nb, nz, *refs):
    (semb, temb, scnt, tcnt, warm, sout, tout,
     S, tt, tt2, warm2, tcnt2, peak, K, W, VT, tsT, part_out, part_in, z_out, z_in,
     ts_out, ts_in, ssem, rsem) = refs
    src = semb.shape[1]
    tgt = temb.shape[1]
    cols = warm.shape[1]
    group = src * nb
    b = lax.axis_index("blk")
    d = lax.axis_index("dom")
    z = d // 2
    c = d % 2
    count = [0]
    f32, bf = jnp.float32, jnp.bfloat16

    core_peer = (b, 2 * z + 1 - c)

    def z_peer(k):
        return (b, 2 * lax.rem(z + k, nz) + c)

    def b_peer(k):
        return (lax.rem(b + k, nb), d)

    started = []

    def send(source, target, device):
        i = count[0]
        count[0] += 1
        copy = pltpu.make_async_remote_copy(
            src_ref=source, dst_ref=target, send_sem=ssem.at[i], recv_sem=rsem.at[i],
            device_id=device, device_id_type=pl.DeviceIdType.MESH)
        copy.start()
        started.append(copy)
        return copy

    def arrived(copies):
        for copy in copies:
            copy.wait_recv()

    barrier = pltpu.get_barrier_semaphore()
    peers = [core_peer] + [z_peer(k) for k in range(1, nz)] + [b_peer(k) for k in range(1, nb)]
    for device in peers:
        pl.semaphore_signal(barrier, inc=1, device_id=device, device_id_type=pl.DeviceIdType.MESH)

    def group_of(i):
        return lax.rem(z - i + nz, nz)

    def block_rows(i):
        return pl.ds(pl.multiple_of((group_of(i) * nb + b) * src, src), src)

    square = nb == 4
    if square:
        y, x = b // 2, b % 2
        first_b = 2 * (y + c * (1 - 2 * y)) + x + (1 - c) * (1 - 2 * x)
        second_b = 2 * (y + (1 - c) * (1 - 2 * y)) + x + c * (1 - 2 * x)
        corner_b = 3 - b

    def gather(from_z, block):
        pending = []
        relays = []

        def spread(i):
            piece = block(i, b)
            if not square:
                pending.append([send(piece, piece, b_peer(j)) for j in range(1, nb)])
                return
            relays.append(send(piece, piece, (first_b, d)))
            pending.append([send(piece, piece, (second_b, d))])

        def relay(i):
            if square:
                relays[i].wait_recv()
                piece = block(i, first_b)
                pending[i].append(send(piece, piece, (second_b, d)))

        spread(0)
        for k in range(1, nz):
            from_z[k - 1].wait_recv()
            spread(k)
            relay(k - 1)
        relay(nz - 1)
        return pending

    def source_block(i, bb):
        return S.at[pl.ds(pl.multiple_of((group_of(i) * nb + bb) * src, src), src)]

    def group_rows(i):
        return pl.ds(pl.multiple_of(group_of(i) * group, group), group)

    scaled = normalized(semb[...]).astype(bf).astype(f32).T * (INV_EPS * LOG2E)
    high = scaled.astype(bf)
    low = (scaled - high.astype(f32)).astype(bf)
    S[block_rows(0), :] = jnp.concatenate([high, low], axis=1)
    peak[0] = jnp.broadcast_to(jnp.max(warm[...], axis=0, keepdims=True), (8, cols))
    unit = normalized(temb[...]).astype(bf)
    tt[...] = jnp.concatenate([unit, unit], axis=0)
    pl.semaphore_wait(barrier, len(peers))

    mine = S.at[block_rows(0)]
    emb_z = [send(mine, mine, z_peer(k)) for k in range(1, nz)]
    peak_z = [send(peak.at[0], peak.at[k], z_peer(k)) for k in range(1, nz)]
    emb_core = send(tt, tt2, core_peer)
    warm_core = send(warm, warm2, core_peer)
    tcnt_core = send(tcnt, tcnt2, core_peer)

    arrived(peak_z)
    top = peak[0]
    for k in range(1, nz):
        top = jnp.maximum(top, peak[k])
    peak[nz] = top
    peak_b = [send(peak.at[nz], peak.at[nz + k], b_peer(k)) for k in range(1, nb)]
    emb_b = gather(emb_z, source_block)
    emb_core.wait_recv()

    width = 256 if tgt % 256 == 0 else 128
    tall = 256 if group % 256 == 0 else 128

    def make_kernel(i):
        base = group_of(i) * group

        def one(step, carry):
            rows = pl.ds(pl.multiple_of(base + step * tall, tall), tall)
            piece = S[rows, :]
            for half, emb in enumerate((tt, tt2)):
                for start in range(0, tgt, width):
                    prod = jnp.dot(piece, emb[:, start:start + width], preferred_element_type=f32)
                    at = half * tgt + start
                    K[rows, at:at + width] = jnp.exp2(prod).astype(bf)
            return carry

        lax.fori_loop(0, group // tall, one, 0)

    arrived(emb_b[0])
    make_kernel(0)
    arrived(peak_b)
    top = peak[nz]
    for k in range(1, nb):
        top = jnp.maximum(top, peak[nz + k])
    peak[nz + nb] = top
    peak_core = send(peak.at[nz + nb], peak.at[nz + nb + 1], core_peer)
    if nz > 1:
        arrived(emb_b[1])
        make_kernel(1)
    warm_core.wait_recv()
    peak_core.wait_recv()
    shift = jnp.maximum(peak[nz + nb], peak[nz + nb + 1])[0:1, :]
    W[0:tgt, :] = jnp.exp(warm[...] - shift).astype(bf)
    W[tgt:2 * tgt, :] = jnp.exp(warm2[...] - shift).astype(bf)

    all_src = src * nb * nz * 2
    all_tgt = tgt * nb * nz * 2

    for it in range(ITERS):
        last = it == ITERS - 1
        to_b = [None] * (nz + 1)

        def rows_of(bb):
            return pl.ds(pl.multiple_of(bb * src, src), src)

        def scatter(i):
            part = part_out.at[it * nz + i % nz]
            part[...] = jnp.dot(K[group_rows(i), :], W[...], preferred_element_type=f32).astype(bf)
            base = (it * nz + i % nz) * (nb - 1)
            if square:
                to_b[i] = [send(part.at[rows_of(corner_b)], part_in.at[base], (second_b, d)),
                           send(part.at[rows_of(second_b)], part_in.at[base + 1], (second_b, d))]
                return
            to_b[i] = []
            for j in range(1, nb):
                to_b[i].append(send(part.at[rows_of(lax.rem(b + j, nb))], part_in.at[base + j - 1], b_peer(j)))

        def combine(i):
            if not square:
                return
            slot = it * nz + i % nz
            to_b[i].pop(0).wait_recv()
            rows = rows_of(first_b)
            both = part_out[slot, rows, :].astype(f32) + part_in[slot * (nb - 1)].astype(f32)
            part_out[slot, rows, :] = both.astype(bf)
            to_b[i].append(send(part_out.at[slot, rows], part_in.at[slot * (nb - 1) + 2], (first_b, d)))

        def summed(i):
            arrived(to_b[i])
            slot = it * nz + i % nz
            total = part_out[slot, rows_of(b), :].astype(f32)
            for j in range(1 if square else 0, nb - 1):
                total = total + part_in[slot * (nb - 1) + j].astype(f32)
            return total

        to_z = []

        def pass_on(i):
            slot = it * nz + i
            z_out[slot] = summed(i).astype(bf)
            to_z.append(send(z_out.at[slot], z_in.at[slot], z_peer(nz - i)))

        for i in range(1, nz + 1):
            if it == 0 and 1 < i < nz:
                arrived(emb_b[i])
                make_kernel(i)
            scatter(i)
            if i > 1:
                combine(i - 1)
            if it == 0 and i > 2:
                pass_on(i - 2)
        if it > 0:
            for i in range(1, nz - 1):
                pass_on(i)
        combine(nz)
        if nz > 1:
            pass_on(nz - 1)
        sums = summed(nz)
        arrived(to_z)
        for i in range(1, nz):
            sums = sums + z_in[it * nz + i].astype(f32)
        counts = scnt[...].astype(f32)
        vt = VT.at[it]

        def weight_block(i, bb):
            return vt.at[group_of(i) * nb + bb]

        vt[group_of(0) * nb + b] = (counts * (1.0 / all_src) / sums).T.astype(bf)
        from_z = [send(weight_block(0, b), weight_block(0, b), z_peer(k)) for k in range(1, nz)]
        from_b = gather(from_z, weight_block)
        if last:
            sout[...] = jnp.log(counts) - math.log(all_src) - shift - (jnp.log(sums) - INV_EPS)
        across = []
        for i in range(nz):
            arrived(from_b[i])
            first = group_of(i) * nb
            lhs = jnp.concatenate([vt[first + j] for j in range(nb)], axis=1)
            for half in (1, 0):
                at = half * tgt
                term = jnp.dot(lhs, K[group_rows(i), at:at + tgt], preferred_element_type=f32)
                if i > 0:
                    term = term + tsT[:, at:at + tgt]
                if i == nz - 1 and (half == 1 or not last):
                    ts_out[it, half] = term.astype(bf)
                    across.append(send(ts_out.at[it, half], ts_in.at[it, 1 - half], core_peer))
                if half == 0 or i < nz - 1 or not last:
                    tsT[:, at:at + tgt] = term
        if last:
            log_counts = jnp.log(tcnt[...].astype(f32))
            arrived(across)
            tsums = (tsT[:, :tgt] + ts_in[it, 0].astype(f32)).T
            tout[...] = log_counts - math.log(all_tgt) + shift - jnp.log(tsums)
        else:
            if it == 0:
                tcnt_core.wait_recv()
            arrived(across)
            for half, held in enumerate((tcnt, tcnt2)):
                at = half * tgt
                tsums = (tsT[:, at:at + tgt] + ts_in[it, half].astype(f32)).T
                W[at:at + tgt, :] = (held[...].astype(f32) * (1.0 / all_tgt) / tsums).astype(bf)
    for copy in started:
        copy.wait_send()


def n_copies(nb, nz):
    gather = (nz - 1) + (nb - 1) * nz
    return gather + (nz - 1) + (nb - 1) + 4 + ITERS * (gather + nz * (nb - 1) + nz - 1 + 1) + ITERS - 1


def place(s_in, t_in, s_out, t_out):
    s_out[...] = s_in[...]
    t_out[...] = t_in[...]


def body(source_emb, target_emb, source_counts, target_counts, warm_start):
    nb = lax.axis_size("blk")
    nz = lax.axis_size("dom") // 2
    src, dim = source_emb.shape
    tgt = target_emb.shape[0]
    cols = warm_start.shape[1]
    group = src * nb
    copies = n_copies(nb, nz)
    bf = jnp.bfloat16
    f32 = jnp.float32
    vmem = pltpu.VMEM
    pairs = group * nz * 2 * tgt
    shapes = (jax.ShapeDtypeStruct((src, cols), f32), jax.ShapeDtypeStruct((tgt, cols), f32))
    results = pl.pallas_call(
        functools.partial(kernel, nb, nz),
        out_shape=shapes,
        in_specs=[pl.BlockSpec(memory_space=pltpu.VMEM)] * 5,
        out_specs=(pl.BlockSpec(memory_space=pltpu.VMEM),) * 2,
        scratch_shapes=[
            vmem((group * nz, 2 * dim), bf),
            vmem((2 * dim, tgt), bf),
            vmem((2 * dim, tgt), bf),
            vmem((tgt, cols), f32),
            vmem((tgt, cols), target_counts.dtype),
            vmem((nz + nb + 2, 8, cols), f32),
            vmem((group * nz, 2 * tgt), bf),
            vmem((2 * tgt, cols), bf),
            vmem((ITERS, nb * nz, cols, src), bf),
            vmem((cols, 2 * tgt), f32),
            vmem((ITERS * nz, group, cols), bf),
            vmem((ITERS * nz * (nb - 1), src, cols), bf),
            vmem((ITERS * nz, src, cols), bf),
            vmem((ITERS * nz, src, cols), bf),
            vmem((ITERS, 2, cols, tgt), bf),
            vmem((ITERS, 2, cols, tgt), bf),
            pltpu.SemaphoreType.DMA((copies,)),
            pltpu.SemaphoreType.DMA((copies,)),
        ],
        cost_estimate=pl.CostEstimate(
            flops=2 * pairs * (dim + 4 * cols), bytes_accessed=2 * 10**6, transcendentals=pairs),
        compiler_params=pltpu.CompilerParams(
            collective_id=0, has_side_effects=True, vmem_limit_bytes=56 * 2**20),
    )(source_emb.T, target_emb.T, source_counts, target_counts, warm_start)
    return pl.pallas_call(
        place,
        out_shape=shapes,
        in_specs=[pl.BlockSpec(memory_space=pltpu.VMEM)] * 2,
        out_specs=(pl.BlockSpec(memory_space=pltpu.VMEM),) * 2,
    )(*results)


def solution(mesh):
    spec = P(("blk", "dom"), None)
    return jax.shard_map(
        body, mesh=mesh, in_specs=(spec,) * 5, out_specs=(spec,) * 2, check_vma=False)
```

```python
import functools
import math

import jax
import jax.numpy as jnp
from jax import lax
from jax.experimental import pallas as pl
from jax.experimental.pallas import tpu as pltpu
from jax.sharding import PartitionSpec as P

ITERS = 2
INV_EPS = 20.0
LOG2E = math.log2(math.e)


def normalized(values):
    widened = values.astype(jnp.float32)
    squared = jnp.sum(widened * widened, axis=0, keepdims=True) + 1e-06
    return widened * lax.rsqrt(squared)


def kernel(nb, nz, *refs):
    (semb, temb, scnt, tcnt, warm, sout, tout,
     S, tt, tt2, warm2, tcnt2, peak, K, W, VT, tsT, part_out, part_in, z_out, z_in,
     ts_out, ts_in, ssem, rsem) = refs
    src = semb.shape[1]
    tgt = temb.shape[1]
    cols = warm.shape[1]
    group = src * nb
    b = lax.axis_index("blk")
    d = lax.axis_index("dom")
    z = d // 2
    c = d % 2
    count = [0]
    f32, bf = jnp.float32, jnp.bfloat16

    core_peer = (b, 2 * z + 1 - c)

    def z_peer(k):
        return (b, 2 * lax.rem(z + k, nz) + c)

    def b_peer(k):
        return (lax.rem(b + k, nb), d)

    started = []

    def send(source, target, device):
        i = count[0]
        count[0] += 1
        copy = pltpu.make_async_remote_copy(
            src_ref=source, dst_ref=target, send_sem=ssem.at[i], recv_sem=rsem.at[i],
            device_id=device, device_id_type=pl.DeviceIdType.MESH)
        copy.start()
        started.append(copy)
        return copy

    def arrived(copies):
        for copy in copies:
            copy.wait_recv()

    barrier = pltpu.get_barrier_semaphore()
    peers = [core_peer] + [z_peer(k) for k in range(1, nz)] + [b_peer(k) for k in range(1, nb)]
    for device in peers:
        pl.semaphore_signal(barrier, inc=1, device_id=device, device_id_type=pl.DeviceIdType.MESH)

    def group_of(i):
        return lax.rem(z - i + nz, nz)

    def block_rows(i):
        return pl.ds(pl.multiple_of((group_of(i) * nb + b) * src, src), src)

    def group_rows(i):
        return pl.ds(pl.multiple_of(group_of(i) * group, group), group)

    scaled = normalized(semb[...]).astype(bf).astype(f32).T * (INV_EPS * LOG2E)
    high = scaled.astype(bf)
    low = (scaled - high.astype(f32)).astype(bf)
    S[block_rows(0), :] = jnp.concatenate([high, low], axis=1)
    peak[0] = jnp.broadcast_to(jnp.max(warm[...], axis=0, keepdims=True), (8, cols))
    unit = normalized(temb[...]).astype(bf)
    tt[...] = jnp.concatenate([unit, unit], axis=0)
    pl.semaphore_wait(barrier, len(peers))

    mine = S.at[block_rows(0)]
    emb_z = [send(mine, mine, z_peer(k)) for k in range(1, nz)]
    peak_z = [send(peak.at[0], peak.at[k], z_peer(k)) for k in range(1, nz)]
    emb_core = send(tt, tt2, core_peer)
    emb_b = [[send(mine, mine, b_peer(j)) for j in range(1, nb)]]
    warm_core = send(warm, warm2, core_peer)
    tcnt_core = send(tcnt, tcnt2, core_peer)

    arrived(peak_z)
    top = peak[0]
    for k in range(1, nz):
        top = jnp.maximum(top, peak[k])
    peak[nz] = top
    peak_b = [send(peak.at[nz], peak.at[nz + k], b_peer(k)) for k in range(1, nb)]
    for k in range(1, nz):
        emb_z[k - 1].wait_recv()
        piece = S.at[block_rows(k)]
        emb_b.append([send(piece, piece, b_peer(j)) for j in range(1, nb)])
    emb_core.wait_recv()

    width = 256 if tgt % 256 == 0 else 128
    tall = 256 if group % 256 == 0 else 128

    def make_kernel(i):
        base = group_of(i) * group

        def one(step, carry):
            rows = pl.ds(pl.multiple_of(base + step * tall, tall), tall)
            piece = S[rows, :]
            for half, emb in enumerate((tt, tt2)):
                for start in range(0, tgt, width):
                    prod = jnp.dot(piece, emb[:, start:start + width], preferred_element_type=f32)
                    at = half * tgt + start
                    K[rows, at:at + width] = jnp.exp2(prod).astype(bf)
            return carry

        lax.fori_loop(0, group // tall, one, 0)

    arrived(emb_b[0])
    make_kernel(0)
    arrived(peak_b)
    top = peak[nz]
    for k in range(1, nb):
        top = jnp.maximum(top, peak[nz + k])
    peak[nz + nb] = top
    peak_core = send(peak.at[nz + nb], peak.at[nz + nb + 1], core_peer)
    if nz > 1:
        arrived(emb_b[1])
        make_kernel(1)
    warm_core.wait_recv()
    peak_core.wait_recv()
    shift = jnp.maximum(peak[nz + nb], peak[nz + nb + 1])[0:1, :]
    W[0:tgt, :] = jnp.exp(warm[...] - shift).astype(bf)
    W[tgt:2 * tgt, :] = jnp.exp(warm2[...] - shift).astype(bf)

    all_src = src * nb * nz * 2
    all_tgt = tgt * nb * nz * 2

    for it in range(ITERS):
        last = it == ITERS - 1
        to_b = [None] * (nz + 1)

        def scatter(i):
            part = part_out.at[it * nz + i % nz]
            part[...] = jnp.dot(K[group_rows(i), :], W[...], preferred_element_type=f32).astype(bf)
            to_b[i] = []
            for j in range(1, nb):
                rows = pl.ds(pl.multiple_of(lax.rem(b + j, nb) * src, src), src)
                to_b[i].append(send(part.at[rows], part_in.at[(it * nz + i % nz) * (nb - 1) + j - 1], b_peer(j)))

        def summed(i):
            arrived(to_b[i])
            slot = it * nz + i % nz
            total = part_out[slot, pl.ds(pl.multiple_of(b * src, src), src), :].astype(f32)
            for j in range(nb - 1):
                total = total + part_in[slot * (nb - 1) + j].astype(f32)
            return total

        to_z = []

        def pass_on(i):
            slot = it * nz + i
            z_out[slot] = summed(i).astype(bf)
            to_z.append(send(z_out.at[slot], z_in.at[slot], z_peer(nz - i)))

        for i in range(1, nz + 1):
            if it == 0 and 1 < i < nz:
                arrived(emb_b[i])
                make_kernel(i)
            scatter(i)
            if it == 0 and i > 2:
                pass_on(i - 2)
        for i in range(max(1, nz - 1) if it == 0 else 1, nz):
            pass_on(i)
        sums = summed(nz)
        arrived(to_z)
        for i in range(1, nz):
            sums = sums + z_in[it * nz + i].astype(f32)
        counts = scnt[...].astype(f32)
        vt = VT.at[it]

        def block(i):
            return vt.at[group_of(i) * nb + b]

        vt[group_of(0) * nb + b] = (counts * (1.0 / all_src) / sums).T.astype(bf)
        from_z = [send(block(0), block(0), z_peer(k)) for k in range(1, nz)]
        from_b = [[send(block(0), block(0), b_peer(j)) for j in range(1, nb)]]
        if last:
            sout[...] = jnp.log(counts) - math.log(all_src) - shift - (jnp.log(sums) - INV_EPS)
        for k in range(1, nz):
            from_z[k - 1].wait_recv()
            from_b.append([send(block(k), block(k), b_peer(j)) for j in range(1, nb)])
        across = []
        for i in range(nz):
            arrived(from_b[i])
            first = group_of(i) * nb
            lhs = jnp.concatenate([vt[first + j] for j in range(nb)], axis=1)
            for half in (1, 0):
                at = half * tgt
                term = jnp.dot(lhs, K[group_rows(i), at:at + tgt], preferred_element_type=f32)
                if i > 0:
                    term = term + tsT[:, at:at + tgt]
                if i == nz - 1 and (half == 1 or not last):
                    ts_out[it, half] = term.astype(bf)
                    across.append(send(ts_out.at[it, half], ts_in.at[it, 1 - half], core_peer))
                if half == 0 or i < nz - 1 or not last:
                    tsT[:, at:at + tgt] = term
        if last:
            log_counts = jnp.log(tcnt[...].astype(f32))
            arrived(across)
            tsums = (tsT[:, :tgt] + ts_in[it, 0].astype(f32)).T
            tout[...] = log_counts - math.log(all_tgt) + shift - jnp.log(tsums)
        else:
            if it == 0:
                tcnt_core.wait_recv()
            arrived(across)
            for half, held in enumerate((tcnt, tcnt2)):
                at = half * tgt
                tsums = (tsT[:, at:at + tgt] + ts_in[it, half].astype(f32)).T
                W[at:at + tgt, :] = (held[...].astype(f32) * (1.0 / all_tgt) / tsums).astype(bf)
    for copy in started:
        copy.wait_send()


def n_copies(nb, nz):
    gather = (nz - 1) + (nb - 1) * nz
    return gather + (nz - 1) + (nb - 1) + 4 + ITERS * (gather + nz * (nb - 1) + nz - 1 + 1) + ITERS - 1


def place(s_in, t_in, s_out, t_out):
    s_out[...] = s_in[...]
    t_out[...] = t_in[...]


def body(source_emb, target_emb, source_counts, target_counts, warm_start):
    nb = lax.axis_size("blk")
    nz = lax.axis_size("dom") // 2
    src, dim = source_emb.shape
    tgt = target_emb.shape[0]
    cols = warm_start.shape[1]
    group = src * nb
    copies = n_copies(nb, nz)
    bf = jnp.bfloat16
    f32 = jnp.float32
    vmem = pltpu.VMEM
    pairs = group * nz * 2 * tgt
    shapes = (jax.ShapeDtypeStruct((src, cols), f32), jax.ShapeDtypeStruct((tgt, cols), f32))
    results = pl.pallas_call(
        functools.partial(kernel, nb, nz),
        out_shape=shapes,
        in_specs=[pl.BlockSpec(memory_space=pltpu.VMEM)] * 5,
        out_specs=(pl.BlockSpec(memory_space=pltpu.VMEM),) * 2,
        scratch_shapes=[
            vmem((group * nz, 2 * dim), bf),
            vmem((2 * dim, tgt), bf),
            vmem((2 * dim, tgt), bf),
            vmem((tgt, cols), f32),
            vmem((tgt, cols), target_counts.dtype),
            vmem((nz + nb + 2, 8, cols), f32),
            vmem((group * nz, 2 * tgt), bf),
            vmem((2 * tgt, cols), bf),
            vmem((ITERS, nb * nz, cols, src), bf),
            vmem((cols, 2 * tgt), f32),
            vmem((ITERS * nz, group, cols), bf),
            vmem((ITERS * nz * (nb - 1), src, cols), bf),
            vmem((ITERS * nz, src, cols), bf),
            vmem((ITERS * nz, src, cols), bf),
            vmem((ITERS, 2, cols, tgt), bf),
            vmem((ITERS, 2, cols, tgt), bf),
            pltpu.SemaphoreType.DMA((copies,)),
            pltpu.SemaphoreType.DMA((copies,)),
        ],
        cost_estimate=pl.CostEstimate(
            flops=2 * pairs * (dim + 4 * cols), bytes_accessed=2 * 10**6, transcendentals=pairs),
        compiler_params=pltpu.CompilerParams(
            collective_id=0, has_side_effects=True, vmem_limit_bytes=56 * 2**20),
    )(source_emb.T, target_emb.T, source_counts, target_counts, warm_start)
    return pl.pallas_call(
        place,
        out_shape=shapes,
        in_specs=[pl.BlockSpec(memory_space=pltpu.VMEM)] * 2,
        out_specs=(pl.BlockSpec(memory_space=pltpu.VMEM),) * 2,
    )(*results)


def solution(mesh):
    spec = P(("blk", "dom"), None)
    return jax.shard_map(
        body, mesh=mesh, in_specs=(spec,) * 5, out_specs=(spec,) * 2, check_vma=False)
```
